32 devices in a mesh: expert: 8 (over z, x), tensor: 4 (over y, core).
Axes of the slice: x: 2, y: 2, z: 4, core: 2. Of those that a mesh axis runs over, the one named last changes fastest.
Arguments:
- routes: int32 [1024, 2], P('expert'), may hold values from 0 to 7, all different within a row; in each aligned block of 128 rows (0 to 127, 128 to 255, ...) at most 40 rows name the same one
- gate_weights: float32 [1024, 2], P('expert'), may hold values from 0.2 to 1
- out_grad: bfloat16 [1024, 3072], P('expert', 'tensor'), may hold values from -6 to 6
- hidden: bfloat16 [8, 320, 6144], P('expert', None, 'tensor'), may hold values from -6 to 6
- down_weight: bfloat16 [8, 6144, 3072], P('expert', 'tensor'), may hold values from -0.078125 to 0.078125
Outputs:
- layer_out: bfloat16 [1024, 3072], P('expert', 'tensor')
- gate_grad: float32 [1024, 2], P('expert')
- hidden_grad: bfloat16 [8, 320, 6144], P('expert', None, 'tensor')
The draws below stay inside these ranges and needn't reach their ends.
Inputs may be any that keep to these rules, and one draw needn't show every extreme that they name: `routes`: each row names 2 different experts. Among the 128 x 2 entries of the rows of one device, no expert is named more than 40 times, a bound that some block reaches there.
All inputs are finite; a program needn't handle non-finite values.
Results may differ from the reference program's by a relative error of at most 0.0051.
Values may be sent and summed in bfloat16 or wider, within the bound.
A program may use at most 64 MiB of HBM per device.

```python
import math
import jax
import jax.numpy as jnp
import numpy as np
from jax import lax

D = 3072
FF = 6144
TOP = 2
TOK_DEV = 128
EXPERTS = 8
CAP = 40
SLOTS = 320
TOKENS = 1024
N_EXPERT = 8


def block_scale(rng, shape, shards, low, largest):
    loudness = 1.0
    for axis_at, parts in shards:
        draws = jax.random.uniform(jax.random.fold_in(jax.random.fold_in(rng, 6), axis_at), (parts,), jnp.float32, low / len(shards), largest / len(shards))
        loudness = loudness * jnp.repeat(jnp.exp(draws), shape[axis_at] // parts).reshape((-1,) + (1,) * (len(shape) - 1 - axis_at))
    return loudness


def shared_out(key, own, number, rows, count, top, limit, lean):
    sequence = jax.random.permutation(key, count)
    heavy_load, common = portions_of(count, rows * top, limit, lean, True), portions_of(count, rows * top, limit, lean, False)
    places = jnp.arange(count)

    def named(tallies, turn):
        used = int((tallies > 0).sum())
        fixed = max(1, used // 4)
        moved = fixed + (places - fixed + turn * (used - fixed)) % max(1, count - fixed)
        return jnp.zeros((count,), jnp.int32).at[sequence[jnp.where(places < fixed, places, moved)]].set(jnp.asarray(tallies, jnp.int32))

    tallies = jnp.where(number % 4 == 0, named(heavy_load, number // 4), named(common, number - number // 4 - 1))
    mixed = jax.random.permutation(jax.random.fold_in(own, 3), count)
    donor, sink = mixed[0:count // 2 * 2:2], mixed[1:count // 2 * 2:2]
    room = jnp.minimum(tallies[donor] - 1, limit - tallies[sink]) // 2
    room = jnp.where((donor == sequence[0]) | (sink == sequence[0]) | (tallies[sink] == 0), 0, jnp.maximum(room, 0))
    moved = jax.random.randint(jax.random.fold_in(own, 4), (count // 2,), 0, 1 << 20) % (room + 1)
    tallies = tallies.at[donor].add(-moved).at[sink].add(moved)
    labels = jnp.searchsorted(jnp.cumsum(tallies), jnp.arange(rows * top), side="right").astype(jnp.int32)
    listing = labels.reshape(top, rows).T
    listing = listing[jax.random.permutation(jax.random.fold_in(own, 1), rows)]
    turn = jax.random.randint(jax.random.fold_in(own, 2), (rows, 1), 0, top)
    return jnp.take_along_axis(listing, (jnp.arange(top)[None, :] + turn) % top, axis=1)


def portions_of(amount, total, reach, lean, full):
    weights = [(1 << 20) // math.isqrt(rank ** lean) + 1 for rank in range(1, amount + 1)]
    largest = reach if full else min(reach, max(-(-total // amount), total * weights[0] // sum(weights)))
    least = 1 if total - largest >= amount - 1 else 0
    given, rest = [largest] + [least] * (amount - 1), total - largest - least * (amount - 1)
    while rest > 0:
        free = [i for i in range(1, amount) if given[i] < largest] or [i for i in range(1, amount) if given[i] < reach]
        whole, budget = sum([weights[i] for i in free]), rest
        for i in free:
            more = min(reach - given[i], max(1, budget * weights[i] // whole), rest)
            given[i] = given[i] + more
            rest = rest - more
    return np.array(given)


def scatter_about(own_key, dims, width, reach, split=(), kind=jnp.bfloat16):
    drawn = width * jax.random.normal(own_key, dims, jnp.float32)
    if split:
        drawn = drawn * block_scale(own_key, dims, split, -0.22, 0.18)
    return jnp.clip(drawn, -reach, reach).astype(kind)


def setup_inputs(seed: int = 0) -> dict:
    keys = jax.random.split(jax.random.key(seed), 6)
    routes_keys = jax.random.split(jax.random.fold_in(keys[0], 1), TOKENS // TOK_DEV)
    routes_turns = jax.random.permutation(jax.random.fold_in(keys[0], 3), TOKENS // TOK_DEV)
    routes = jax.vmap(lambda own, number: shared_out(jax.random.fold_in(keys[0], 2), own, number, TOK_DEV, EXPERTS, TOP, CAP, 2))(routes_keys, routes_turns).reshape((TOKENS, TOP))
    gate_weights = jnp.clip(0.2 + 0.8 * jax.random.uniform(keys[1], (TOKENS, TOP), jnp.float32) ** block_scale(keys[1], (TOKENS, TOP), ((0, 8),), -0.2, 0.2), 0.2, 1.0)
    out_grad = scatter_about(keys[2], (TOKENS, D), 1.0, 6.0, ((0, 8), (1, 4)))
    hidden = scatter_about(keys[3], (EXPERTS, SLOTS, FF), 1.0, 6.0, ((0, 8), (2, 4)))
    down_weight = scatter_about(keys[4], (EXPERTS, FF, D), FF ** -0.5, 0.078125, ((0, 8), (1, 4)))
    return {"routes": routes, "gate_weights": gate_weights, "out_grad": out_grad, "hidden": hidden, "down_weight": down_weight}


def expert_forward(operands):
    return jnp.dot(operands[0], operands[1], preferred_element_type=jnp.float32).astype(jnp.bfloat16)


def expert_backward(operands):
    return jnp.dot(operands[0], operands[1].T, preferred_element_type=jnp.float32).astype(jnp.bfloat16)


def reference(routes, gate_weights, out_grad, hidden, down_weight):
    blocks = routes.reshape(N_EXPERT, TOK_DEV * TOP)
    onehot = (blocks[:, :, None] == jnp.arange(EXPERTS, dtype=jnp.int32)[None, None, :]).astype(jnp.int32)
    before = jnp.cumsum(onehot, axis=1) - onehot
    position = jnp.sum(before * onehot, axis=2)
    source = jnp.arange(N_EXPERT, dtype=jnp.int32)[:, None]
    slot_index = (source * CAP + position).reshape(TOKENS, TOP).astype(jnp.int32)
    expert_out = lax.map(expert_forward, (hidden, down_weight))
    chosen = expert_out[routes, slot_index].astype(jnp.float32)
    layer_out = jnp.sum(gate_weights[:, :, None] * chosen, axis=1).astype(jnp.bfloat16)
    cotangent = out_grad.astype(jnp.float32)
    gate_grad = jnp.sum(cotangent[:, None, :] * chosen, axis=2)
    scaled = (gate_weights[:, :, None] * cotangent[:, None, :]).astype(jnp.bfloat16)
    dispatched = jnp.zeros((EXPERTS, SLOTS, D), jnp.bfloat16).at[routes, slot_index].set(scaled)
    hidden_grad = lax.map(expert_backward, (dispatched, down_weight))
    return layer_out, gate_grad, hidden_grad
```

```python
import jax
import jax.numpy as jnp
from jax import lax
from jax.experimental import pallas as pl
from jax.experimental.pallas import tpu as pltpu
from jax.sharding import PartitionSpec as P

BF16, F32 = jnp.bfloat16, jnp.float32
FAR_FIRST = (4, 3, 5, 2, 6, 1, 7, 0)
NEAR_FIRST = (0, 1, 7, 2, 6, 3, 5, 4)


def plain(routes, gate_weights, out_grad, hidden, down_weight):
    sources = lax.axis_size("expert")
    slots = hidden.shape[1]
    capacity = slots // sources
    weight = down_weight[0]
    flat = routes.reshape(-1)
    onehot = (flat[:, None] == jnp.arange(sources, dtype=jnp.int32)[None, :]).astype(jnp.int32)
    position = jnp.sum((jnp.cumsum(onehot, axis=0) - onehot) * onehot, axis=1)
    column = (flat * capacity + position).reshape(routes.shape)
    marks = column[:, :, None] == jnp.arange(slots, dtype=jnp.int32)[None, None, :]
    marks_half = marks.astype(jnp.bfloat16)
    picker = jnp.sum(marks.astype(jnp.float32), axis=1).astype(jnp.bfloat16)
    slot_gate = jnp.sum(gate_weights[:, :, None] * marks.astype(jnp.float32), axis=(0, 1))
    columns = weight
    summed = lax.psum_scatter(
        lax.dot_general(
            columns, hidden[0], (((0,), (1,)), ((), ())), preferred_element_type=jnp.float32
        ),
        "tensor",
        scatter_dimension=0,
        tiled=True,
    )
    outgoing = summed.astype(jnp.bfloat16)
    picked = lax.dot_general(
        out_grad, picker, (((0,), (0,)), ((), ())), preferred_element_type=jnp.float32
    )
    to_send = (picked * slot_gate[None, :]).astype(jnp.bfloat16)
    returned = lax.all_to_all(outgoing, "expert", split_axis=1, concat_axis=1, tiled=True)
    arrived = lax.all_to_all(to_send, "expert", split_axis=1, concat_axis=1, tiled=True)
    chosen = lax.dot_general(
        marks_half, returned, (((2,), (1,)), ((), ())), preferred_element_type=jnp.float32
    )
    layer_out = jnp.sum(gate_weights[:, :, None] * chosen, axis=1).astype(jnp.bfloat16)
    own_terms = jnp.sum(out_grad.astype(jnp.float32)[:, None, :] * chosen, axis=2)
    gate_grad = lax.psum(own_terms, "tensor")
    columns = weight
    grad_sum = lax.dot_general(
        lax.all_gather(arrived, "tensor", axis=0, tiled=True),
        columns,
        (((0,), (1,)), ((), ())),
        preferred_element_type=jnp.float32,
    )
    hidden_grad = grad_sum.astype(jnp.bfloat16)[None]
    return (layer_out, gate_grad, hidden_grad)


def fused_kernel(
    routes_ref, gates_ref, out_grad_ref, hidden_hbm, weight_hbm,
    layer_ref, gate_grad_ref, hidden_grad_ref,
    hidden, weight, partial, core_out, core_in, y_out, y_in,
    slots_out, returned, tokens_out, gathered, total, terms,
    load_sem, core_send, core_recv, y_send, y_recv, out_send, out_recv,
    tok_send, tok_recv, gc_send, gc_recv, gy_send, gy_recv, gf_send, gf_recv,
    term_send, term_recv,
):
    experts, rows2, half = returned.shape
    cap = rows2 // 2
    slots = experts * cap
    own = lax.axis_index("expert")
    rank = lax.axis_index("tensor")
    chip, core = rank // 2, rank % 2
    sibling = chip * 2 + (1 - core)
    across = (1 - chip) * 2 + core
    diagonal = (1 - chip) * 2 + (1 - core)
    width = 2 * half

    def send(source, target, send_sem, recv_sem, expert, tensor):
        return pltpu.make_async_remote_copy(
            src_ref=source, dst_ref=target, send_sem=send_sem, recv_sem=recv_sem,
            device_id=(expert, tensor), device_id_type=pl.DeviceIdType.MESH,
        )

    loads = [pltpu.make_async_copy(hidden_hbm.at[0], hidden, load_sem.at[4])]
    for j, group in enumerate((diagonal, across, sibling, rank)):
        columns = pl.ds(pl.multiple_of(group * width, width), width)
        loads.append(pltpu.make_async_copy(
            weight_hbm.at[0, :, columns], weight.at[j], load_sem.at[j]))
    for load in loads:
        load.start()

    barrier = pltpu.get_barrier_semaphore()
    for i in range(1, experts):
        pl.semaphore_signal(barrier, inc=1, device_id=((own + i) % experts, rank),
                            device_id_type=pl.DeviceIdType.MESH)
    for peer in (sibling, across, diagonal):
        pl.semaphore_signal(barrier, inc=1, device_id=(own, peer),
                            device_id_type=pl.DeviceIdType.MESH)

    def pack(values):
        left = values[:, :half].reshape(experts, cap, half)
        right = values[:, half:].reshape(experts, cap, half)
        return jnp.concatenate([left, right], axis=1)

    def unpack(values):
        values = values.astype(F32)
        both = jnp.concatenate([values[:, :cap], values[:, cap:]], axis=2)
        return both.reshape(slots, width).astype(BF16)

    routes = routes_ref[...]
    gates = gates_ref[...]
    tokens = routes.shape[1]
    expert_id = lax.broadcasted_iota(jnp.int32, (experts, tokens), 0)
    named = [(expert_id == routes[k:k + 1]).astype(F32) for k in range(2)]
    earlier = (lax.broadcasted_iota(jnp.int32, (tokens, tokens), 0)
               < lax.broadcasted_iota(jnp.int32, (tokens, tokens), 1))
    before = jnp.dot((named[0] + named[1]).astype(BF16), earlier.astype(F32).astype(BF16),
                     preferred_element_type=F32)
    slot_id = lax.broadcasted_iota(jnp.int32, (slots, tokens), 0)
    marks = []
    for k in range(2):
        position = jnp.sum(before * named[k], axis=0, keepdims=True).astype(jnp.int32)
        marks.append((slot_id == routes[k:k + 1] * cap + position).astype(F32))
    slot_gate = jnp.sum(marks[0] * gates[0:1] + marks[1] * gates[1:2], axis=1, keepdims=True)
    picked = jnp.dot((marks[0] + marks[1]).astype(BF16), out_grad_ref[...],
                     preferred_element_type=F32)
    tokens_out[...] = pack(picked * slot_gate).astype(BF16)

    pl.semaphore_wait(barrier, experts - 1 + 3)

    sends = []
    token_copies = {}
    for i in FAR_FIRST[:-1]:
        expert = (own + i) % experts
        token_copies[i] = send(tokens_out.at[expert], gathered.at[0, own],
                               tok_send.at[i], tok_recv.at[i], expert, rank)
        token_copies[i].start()
    gathered[0, own] = tokens_out[own]

    def product(j):
        return pack(jnp.dot(hidden[...], weight[j], preferred_element_type=F32))

    loads[0].wait()
    loads[1].wait()
    core_out[0] = product(0).astype(BF16)
    to_core = [send(core_out.at[n], core_in.at[n], core_send.at[n], core_recv.at[n], own, sibling)
               for n in range(2)]
    to_core[0].start()
    loads[2].wait()
    partial[...] = product(1)
    to_core[0].wait_recv()
    to_y = {}
    for i in FAR_FIRST:
        expert = (own + i) % experts
        y_out[expert] = (partial[expert] + core_in[0, expert].astype(F32)).astype(BF16)
        to_y[i] = send(y_out.at[expert], y_in.at[expert], y_send.at[i], y_recv.at[i], own, across)
        to_y[i].start()
    loads[3].wait()
    core_out[1] = product(2).astype(BF16)
    to_core[1].start()
    loads[4].wait()
    partial[...] = product(3)
    to_core[1].wait_recv()
    partial[...] = partial[...] + core_in[1].astype(F32)

    to_slots, to_sibling, to_across, onward = {}, {}, {}, {}
    for far, near in zip(FAR_FIRST, NEAR_FIRST):
        source = (own - near + experts) % experts
        if near:
            token_copies[near].wait_recv()
        to_across[near] = send(gathered.at[0, source], gathered.at[2, source],
                               gy_send.at[near], gy_recv.at[near], own, across)
        to_across[near].start()
        to_sibling[near] = send(gathered.at[0, source], gathered.at[1, source],
                                gc_send.at[near], gc_recv.at[near], own, sibling)
        to_sibling[near].start()

        expert = (own + far) % experts
        to_y[far].wait_recv()
        block = (partial[expert] + y_in[expert].astype(F32)).astype(BF16)
        if far:
            slots_out[expert] = block
            to_slots[far] = send(slots_out.at[expert], returned.at[own],
                                 out_send.at[far], out_recv.at[far], expert, rank)
            to_slots[far].start()
        else:
            returned[own] = block

    def back(part, j):
        return lax.dot_general(unpack(gathered[part]), weight[j], (((1,), (1,)), ((), ())),
                               preferred_element_type=F32)

    total[...] = back(0, 3)
    for near in NEAR_FIRST:
        to_sibling[near].wait_recv()
    total[...] = total[...] + back(1, 2)
    for near in NEAR_FIRST:
        source = (own - near + experts) % experts
        to_across[near].wait_recv()
        onward[near] = send(gathered.at[2, source], gathered.at[3, source],
                            gf_send.at[near], gf_recv.at[near], own, sibling)
        onward[near].start()
    total[...] = total[...] + back(2, 1)

    for far in FAR_FIRST[:-1]:
        to_slots[far].wait_recv()
    outputs = unpack(returned[...])
    cotangent = out_grad_ref[...].astype(F32)
    layer = jnp.zeros((tokens, width), F32)
    lane = lax.broadcasted_iota(jnp.int32, (tokens, tokens), 1)
    spread = jnp.zeros((tokens, tokens), F32)
    for k in range(2):
        chosen = jnp.dot(marks[k].T.astype(BF16), outputs, preferred_element_type=F32)
        gate = jnp.broadcast_to(gates[k:k + 1], (tokens, tokens)).T[:, :1]
        layer = layer + gate * chosen
        term = jnp.sum(cotangent * chosen, axis=1, keepdims=True)
        spread = spread + jnp.where(lane == k, term, 0.0)
    layer_ref[...] = layer.astype(BF16)
    terms[rank] = spread.T[:8]
    to_terms = []
    for n, peer in enumerate((sibling, across, diagonal)):
        to_terms.append(send(terms.at[rank], terms.at[rank], term_send.at[n], term_recv.at[n],
                             own, peer))
        to_terms[n].start()

    for near in NEAR_FIRST:
        onward[near].wait_recv()
    hidden_grad_ref[0] = (total[...] + back(3, 0)).astype(BF16)

    for copy in to_terms:
        copy.wait_recv()
    gate_grad_ref[...] = (terms[0] + terms[1] + terms[2] + terms[3])[:2]

    for group in (token_copies, to_y, to_slots, to_sibling, to_across, onward):
        for copy in group.values():
            copy.wait_send()
    for copy in to_core + to_terms:
        copy.wait_send()


def fused(routes, gate_weights, out_grad, hidden, down_weight):
    experts = lax.axis_size("expert")
    _, slots, depth = hidden.shape
    tokens, width = out_grad.shape
    blocks = (experts, 2 * slots // experts, width // 2)
    vmem = pl.BlockSpec(memory_space=pltpu.VMEM)
    hbm = pl.BlockSpec(memory_space=pl.ANY)
    sems = lambda n: pltpu.SemaphoreType.DMA((n,))
    layer_out, gate_grad, hidden_grad = pl.pallas_call(
        fused_kernel,
        out_shape=(
            jax.ShapeDtypeStruct((tokens, width), BF16),
            jax.ShapeDtypeStruct((2, tokens), F32),
            jax.ShapeDtypeStruct((1, slots, depth), BF16),
        ),
        in_specs=[vmem, vmem, vmem, hbm, hbm],
        out_specs=(vmem, vmem, vmem),
        scratch_shapes=[
            pltpu.VMEM((slots, depth), BF16),
            pltpu.VMEM((4, depth, width), BF16),
            pltpu.VMEM(blocks, F32),
            pltpu.VMEM((2,) + blocks, BF16),
            pltpu.VMEM((2,) + blocks, BF16),
            pltpu.VMEM(blocks, BF16),
            pltpu.VMEM(blocks, BF16),
            pltpu.VMEM(blocks, BF16),
            pltpu.VMEM(blocks, BF16),
            pltpu.VMEM(blocks, BF16),
            pltpu.VMEM((4,) + blocks, BF16),
            pltpu.VMEM((slots, depth), F32),
            pltpu.VMEM((4, 8, tokens), F32),
            sems(5), sems(2), sems(2),
        ] + [sems(8)] * 12 + [sems(3), sems(3)],
        compiler_params=pltpu.CompilerParams(
            collective_id=0, has_side_effects=True, vmem_limit_bytes=56 * 1024 * 1024
        ),
        cost_estimate=pl.CostEstimate(
            flops=16 * slots * depth * width, bytes_accessed=8 * depth * width, transcendentals=0
        ),
    )(routes.T, gate_weights.T, out_grad, hidden, down_weight)
    return layer_out, gate_grad.T, hidden_grad


def per_device(routes, gate_weights, out_grad, hidden, down_weight):
    experts, ranks = lax.axis_size("expert"), lax.axis_size("tensor")
    cap = hidden.shape[1] // experts
    fits = (experts == 8 and ranks == 4 and cap % 8 == 0 and routes.shape == (128, 2)
            and out_grad.shape[1] % 256 == 0 and hidden.shape[2] % 128 == 0)
    chosen = fused if fits else plain
    return chosen(routes, gate_weights, out_grad, hidden, down_weight)


def solution(mesh):
    return jax.shard_map(
        per_device,
        mesh=mesh,
        in_specs=(
            P("expert", None),
            P("expert", None),
            P("expert", "tensor"),
            P("expert", None, "tensor"),
            P("expert", "tensor", None),
        ),
        out_specs=(P("expert", "tensor"), P("expert", None), P("expert", None, "tensor")),
        check_vma=False,
    )
```

```python
import jax
import jax.numpy as jnp
from jax import lax
from jax.experimental import pallas as pl
from jax.experimental.pallas import tpu as pltpu
from jax.sharding import PartitionSpec as P

BF16, F32 = jnp.bfloat16, jnp.float32
FAR_FIRST = (4, 5, 6, 7, 2, 3, 1, 0)
NEAR_FIRST = (0, 1, 2, 3, 6, 7, 4, 5)


def plain(routes, gate_weights, out_grad, hidden, down_weight):
    sources = lax.axis_size("expert")
    slots = hidden.shape[1]
    capacity = slots // sources
    weight = down_weight[0]
    flat = routes.reshape(-1)
    onehot = (flat[:, None] == jnp.arange(sources, dtype=jnp.int32)[None, :]).astype(jnp.int32)
    position = jnp.sum((jnp.cumsum(onehot, axis=0) - onehot) * onehot, axis=1)
    column = (flat * capacity + position).reshape(routes.shape)
    marks = column[:, :, None] == jnp.arange(slots, dtype=jnp.int32)[None, None, :]
    marks_half = marks.astype(jnp.bfloat16)
    picker = jnp.sum(marks.astype(jnp.float32), axis=1).astype(jnp.bfloat16)
    slot_gate = jnp.sum(gate_weights[:, :, None] * marks.astype(jnp.float32), axis=(0, 1))
    columns = weight
    summed = lax.psum_scatter(
        lax.dot_general(
            columns, hidden[0], (((0,), (1,)), ((), ())), preferred_element_type=jnp.float32
        ),
        "tensor",
        scatter_dimension=0,
        tiled=True,
    )
    outgoing = summed.astype(jnp.bfloat16)
    picked = lax.dot_general(
        out_grad, picker, (((0,), (0,)), ((), ())), preferred_element_type=jnp.float32
    )
    to_send = (picked * slot_gate[None, :]).astype(jnp.bfloat16)
    returned = lax.all_to_all(outgoing, "expert", split_axis=1, concat_axis=1, tiled=True)
    arrived = lax.all_to_all(to_send, "expert", split_axis=1, concat_axis=1, tiled=True)
    chosen = lax.dot_general(
        marks_half, returned, (((2,), (1,)), ((), ())), preferred_element_type=jnp.float32
    )
    layer_out = jnp.sum(gate_weights[:, :, None] * chosen, axis=1).astype(jnp.bfloat16)
    own_terms = jnp.sum(out_grad.astype(jnp.float32)[:, None, :] * chosen, axis=2)
    gate_grad = lax.psum(own_terms, "tensor")
    columns = weight
    grad_sum = lax.dot_general(
        lax.all_gather(arrived, "tensor", axis=0, tiled=True),
        columns,
        (((0,), (1,)), ((), ())),
        preferred_element_type=jnp.float32,
    )
    hidden_grad = grad_sum.astype(jnp.bfloat16)[None]
    return (layer_out, gate_grad, hidden_grad)


def fused_kernel(
    routes_ref, gates_ref, out_grad_ref, hidden_hbm, weight_hbm,
    layer_ref, gate_grad_ref, hidden_grad_ref,
    hidden, weight, partial, core_out, core_in, y_out, y_in,
    slots_out, returned, tokens_out, gathered, total, terms,
    load_sem, core_send, core_recv, y_send, y_recv, out_send, out_recv,
    tok_send, tok_recv, gc_send, gc_recv, gy_send, gy_recv, gf_send, gf_recv,
    term_send, term_recv,
):
    experts, rows2, half = returned.shape
    cap = rows2 // 2
    slots = experts * cap
    own = lax.axis_index("expert")
    rank = lax.axis_index("tensor")
    chip, core = rank // 2, rank % 2
    sibling = chip * 2 + (1 - core)
    across = (1 - chip) * 2 + core
    diagonal = (1 - chip) * 2 + (1 - core)
    width = 2 * half

    def partner(i):
        index = own
        for bit in (1, 2, 4):
            if i & bit:
                index = index + bit * (1 - 2 * ((own // bit) % 2))
        return index

    def send(source, target, send_sem, recv_sem, expert, tensor):
        return pltpu.make_async_remote_copy(
            src_ref=source, dst_ref=target, send_sem=send_sem, recv_sem=recv_sem,
            device_id=(expert, tensor), device_id_type=pl.DeviceIdType.MESH,
        )

    loads = [pltpu.make_async_copy(hidden_hbm.at[0], hidden, load_sem.at[4])]
    for j, group in enumerate((diagonal, across, sibling, rank)):
        columns = pl.ds(pl.multiple_of(group * width, width), width)
        loads.append(pltpu.make_async_copy(
            weight_hbm.at[0, :, columns], weight.at[j], load_sem.at[j]))
    for load in loads:
        load.start()

    barrier = pltpu.get_barrier_semaphore()
    for i in range(1, experts):
        pl.semaphore_signal(barrier, inc=1, device_id=(partner(i), rank),
                            device_id_type=pl.DeviceIdType.MESH)
    for peer in (sibling, across, diagonal):
        pl.semaphore_signal(barrier, inc=1, device_id=(own, peer),
                            device_id_type=pl.DeviceIdType.MESH)

    def pack(values):
        left = values[:, :half].reshape(experts, cap, half)
        right = values[:, half:].reshape(experts, cap, half)
        return jnp.concatenate([left, right], axis=1)

    def unpack(values):
        values = values.astype(F32)
        both = jnp.concatenate([values[:, :cap], values[:, cap:]], axis=2)
        return both.reshape(slots, width).astype(BF16)

    routes = routes_ref[...]
    gates = gates_ref[...]
    tokens = routes.shape[1]
    expert_id = lax.broadcasted_iota(jnp.int32, (experts, tokens), 0)
    named = [(expert_id == routes[k:k + 1]).astype(F32) for k in range(2)]
    earlier = (lax.broadcasted_iota(jnp.int32, (tokens, tokens), 0)
               < lax.broadcasted_iota(jnp.int32, (tokens, tokens), 1))
    before = jnp.dot((named[0] + named[1]).astype(BF16), earlier.astype(F32).astype(BF16),
                     preferred_element_type=F32)
    slot_id = lax.broadcasted_iota(jnp.int32, (slots, tokens), 0)
    marks = []
    for k in range(2):
        position = jnp.sum(before * named[k], axis=0, keepdims=True).astype(jnp.int32)
        marks.append((slot_id == routes[k:k + 1] * cap + position).astype(F32))
    slot_gate = jnp.sum(marks[0] * gates[0:1] + marks[1] * gates[1:2], axis=1, keepdims=True)
    picked = jnp.dot((marks[0] + marks[1]).astype(BF16), out_grad_ref[...],
                     preferred_element_type=F32)
    tokens_out[...] = pack(picked * slot_gate).astype(BF16)

    pl.semaphore_wait(barrier, experts - 1 + 3)

    sends = []
    token_copies = {}
    for i in FAR_FIRST[:-1]:
        expert = partner(i)
        token_copies[i] = send(tokens_out.at[expert], gathered.at[0, own],
                               tok_send.at[i], tok_recv.at[i], expert, rank)
        token_copies[i].start()
    gathered[0, own] = tokens_out[own]

    to_slots, to_sibling, to_across, onward = {}, {}, {}, {}

    def share(near):
        source = partner(near)
        if near:
            token_copies[near].wait_recv()
        to_across[near] = send(gathered.at[0, source], gathered.at[2, source],
                               gy_send.at[near], gy_recv.at[near], own, across)
        to_across[near].start()
        to_sibling[near] = send(gathered.at[0, source], gathered.at[1, source],
                                gc_send.at[near], gc_recv.at[near], own, sibling)
        to_sibling[near].start()

    share(0)

    def product(j):
        return pack(jnp.dot(hidden[...], weight[j], preferred_element_type=F32))

    loads[0].wait()
    loads[1].wait()
    core_out[0] = product(0).astype(BF16)
    to_core = [send(core_out.at[n], core_in.at[n], core_send.at[n], core_recv.at[n], own, sibling)
               for n in range(2)]
    to_core[0].start()
    share(1)
    loads[2].wait()
    partial[...] = product(1)
    share(2)
    to_core[0].wait_recv()
    to_y = {}
    for i in FAR_FIRST:
        expert = partner(i)
        y_out[expert] = (partial[expert] + core_in[0, expert].astype(F32)).astype(BF16)
        to_y[i] = send(y_out.at[expert], y_in.at[expert], y_send.at[i], y_recv.at[i], own, across)
        to_y[i].start()
    loads[3].wait()
    core_out[1] = product(2).astype(BF16)
    to_core[1].start()
    share(3)
    loads[4].wait()
    partial[...] = product(3)
    to_core[1].wait_recv()
    partial[...] = partial[...] + core_in[1].astype(F32)

    for step, far in enumerate(FAR_FIRST):
        expert = partner(far)
        to_y[far].wait_recv()
        block = (partial[expert] + y_in[expert].astype(F32)).astype(BF16)
        if far:
            slots_out[expert] = block
            to_slots[far] = send(slots_out.at[expert], returned.at[own],
                                 out_send.at[far], out_recv.at[far], expert, rank)
            to_slots[far].start()
        else:
            returned[own] = block
        if step % 2:
            share(NEAR_FIRST[4 + step // 2])

    def back(part, j):
        return lax.dot_general(unpack(gathered[part]), weight[j], (((1,), (1,)), ((), ())),
                               preferred_element_type=F32)

    total[...] = back(0, 3)
    for near in NEAR_FIRST:
        to_sibling[near].wait_recv()
    total[...] = total[...] + back(1, 2)
    for near in NEAR_FIRST:
        source = partner(near)
        to_across[near].wait_recv()
        onward[near] = send(gathered.at[2, source], gathered.at[3, source],
                            gf_send.at[near], gf_recv.at[near], own, sibling)
        onward[near].start()
    total[...] = total[...] + back(2, 1)

    for far in FAR_FIRST[:-1]:
        to_slots[far].wait_recv()
    outputs = unpack(returned[...])
    cotangent = out_grad_ref[...].astype(F32)
    layer = jnp.zeros((tokens, width), F32)
    lane = lax.broadcasted_iota(jnp.int32, (tokens, tokens), 1)
    spread = jnp.zeros((tokens, tokens), F32)
    for k in range(2):
        chosen = jnp.dot(marks[k].T.astype(BF16), outputs, preferred_element_type=F32)
        gate = jnp.broadcast_to(gates[k:k + 1], (tokens, tokens)).T[:, :1]
        layer = layer + gate * chosen
        term = jnp.sum(cotangent * chosen, axis=1, keepdims=True)
        spread = spread + jnp.where(lane == k, term, 0.0)
    layer_ref[...] = layer.astype(BF16)
    terms[rank] = spread.T[:8]
    to_terms = []
    for n, peer in enumerate((sibling, across, diagonal)):
        to_terms.append(send(terms.at[rank], terms.at[rank], term_send.at[n], term_recv.at[n],
                             own, peer))
        to_terms[n].start()

    for near in NEAR_FIRST:
        onward[near].wait_recv()
    hidden_grad_ref[0] = (total[...] + back(3, 0)).astype(BF16)

    for copy in to_terms:
        copy.wait_recv()
    gate_grad_ref[...] = (terms[0] + terms[1] + terms[2] + terms[3])[:2]

    for group in (token_copies, to_y, to_slots, to_sibling, to_across, onward):
        for copy in group.values():
            copy.wait_send()
    for copy in to_core + to_terms:
        copy.wait_send()


def hand_over_kernel(layer_in, gate_in, grad_in, layer_ref, gate_ref, grad_ref):
    layer_ref[...] = layer_in[...]
    gate_ref[...] = gate_in[...]
    grad_ref[...] = grad_in[...]


def hand_over(*arrays):
    vmem = pl.BlockSpec(memory_space=pltpu.VMEM)
    return pl.pallas_call(
        hand_over_kernel,
        out_shape=tuple(jax.ShapeDtypeStruct(a.shape, a.dtype) for a in arrays),
        in_specs=[vmem] * 3,
        out_specs=(vmem,) * 3,
        compiler_params=pltpu.CompilerParams(vmem_limit_bytes=16 * 1024 * 1024),
    )(*arrays)


def fused(routes, gate_weights, out_grad, hidden, down_weight):
    experts = lax.axis_size("expert")
    _, slots, depth = hidden.shape
    tokens, width = out_grad.shape
    blocks = (experts, 2 * slots // experts, width // 2)
    vmem = pl.BlockSpec(memory_space=pltpu.VMEM)
    hbm = pl.BlockSpec(memory_space=pl.ANY)
    sems = lambda n: pltpu.SemaphoreType.DMA((n,))
    layer_out, gate_grad, hidden_grad = pl.pallas_call(
        fused_kernel,
        out_shape=(
            jax.ShapeDtypeStruct((tokens, width), BF16),
            jax.ShapeDtypeStruct((2, tokens), F32),
            jax.ShapeDtypeStruct((1, slots, depth), BF16),
        ),
        in_specs=[vmem, vmem, vmem, hbm, hbm],
        out_specs=(vmem, vmem, vmem),
        scratch_shapes=[
            pltpu.VMEM((slots, depth), BF16),
            pltpu.VMEM((4, depth, width), BF16),
            pltpu.VMEM(blocks, F32),
            pltpu.VMEM((2,) + blocks, BF16),
            pltpu.VMEM((2,) + blocks, BF16),
            pltpu.VMEM(blocks, BF16),
            pltpu.VMEM(blocks, BF16),
            pltpu.VMEM(blocks, BF16),
            pltpu.VMEM(blocks, BF16),
            pltpu.VMEM(blocks, BF16),
            pltpu.VMEM((4,) + blocks, BF16),
            pltpu.VMEM((slots, depth), F32),
            pltpu.VMEM((4, 8, tokens), F32),
            sems(5), sems(2), sems(2),
        ] + [sems(8)] * 12 + [sems(3), sems(3)],
        compiler_params=pltpu.CompilerParams(
            collective_id=0, has_side_effects=True, vmem_limit_bytes=52 * 1024 * 1024
        ),
        cost_estimate=pl.CostEstimate(
            flops=16 * slots * depth * width, bytes_accessed=8 * depth * width, transcendentals=0
        ),
    )(routes.T, gate_weights.T, out_grad, hidden, down_weight)
    layer_out, gate_grad, hidden_grad = hand_over(layer_out, gate_grad, hidden_grad)
    return layer_out, gate_grad.T, hidden_grad


def per_device(routes, gate_weights, out_grad, hidden, down_weight):
    experts, ranks = lax.axis_size("expert"), lax.axis_size("tensor")
    cap = hidden.shape[1] // experts
    fits = (experts == 8 and ranks == 4 and cap % 8 == 0 and routes.shape == (128, 2)
            and out_grad.shape[1] % 256 == 0 and hidden.shape[2] % 128 == 0)
    chosen = fused if fits else plain
    return chosen(routes, gate_weights, out_grad, hidden, down_weight)


def solution(mesh):
    return jax.shard_map(
        per_device,
        mesh=mesh,
        in_specs=(
            P("expert", None),
            P("expert", None),
            P("expert", "tensor"),
            P("expert", None, "tensor"),
            P("expert", "tensor", None),
        ),
        out_specs=(P("expert", "tensor"), P("expert", None), P("expert", None, "tensor")),
        check_vma=False,
    )
```

```python
import jax
import jax.numpy as jnp
from jax import lax
from jax.experimental import pallas as pl
from jax.experimental.pallas import tpu as pltpu
from jax.sharding import PartitionSpec as P

BF16, F32 = jnp.bfloat16, jnp.float32
FAR_FIRST = (4, 5, 6, 7, 2, 3, 1, 0)
NEAR_FIRST = (0, 1, 2, 3, 6, 7, 4, 5)


def plain(routes, gate_weights, out_grad, hidden, down_weight):
    sources = lax.axis_size("expert")
    slots = hidden.shape[1]
    capacity = slots // sources
    weight = down_weight[0]
    flat = routes.reshape(-1)
    onehot = (flat[:, None] == jnp.arange(sources, dtype=jnp.int32)[None, :]).astype(jnp.int32)
    position = jnp.sum((jnp.cumsum(onehot, axis=0) - onehot) * onehot, axis=1)
    column = (flat * capacity + position).reshape(routes.shape)
    marks = column[:, :, None] == jnp.arange(slots, dtype=jnp.int32)[None, None, :]
    marks_half = marks.astype(jnp.bfloat16)
    picker = jnp.sum(marks.astype(jnp.float32), axis=1).astype(jnp.bfloat16)
    slot_gate = jnp.sum(gate_weights[:, :, None] * marks.astype(jnp.float32), axis=(0, 1))
    columns = weight
    summed = lax.psum_scatter(
        lax.dot_general(
            columns, hidden[0], (((0,), (1,)), ((), ())), preferred_element_type=jnp.float32
        ),
        "tensor",
        scatter_dimension=0,
        tiled=True,
    )
    outgoing = summed.astype(jnp.bfloat16)
    picked = lax.dot_general(
        out_grad, picker, (((0,), (0,)), ((), ())), preferred_element_type=jnp.float32
    )
    to_send = (picked * slot_gate[None, :]).astype(jnp.bfloat16)
    returned = lax.all_to_all(outgoing, "expert", split_axis=1, concat_axis=1, tiled=True)
    arrived = lax.all_to_all(to_send, "expert", split_axis=1, concat_axis=1, tiled=True)
    chosen = lax.dot_general(
        marks_half, returned, (((2,), (1,)), ((), ())), preferred_element_type=jnp.float32
    )
    layer_out = jnp.sum(gate_weights[:, :, None] * chosen, axis=1).astype(jnp.bfloat16)
    own_terms = jnp.sum(out_grad.astype(jnp.float32)[:, None, :] * chosen, axis=2)
    gate_grad = lax.psum(own_terms, "tensor")
    columns = weight
    grad_sum = lax.dot_general(
        lax.all_gather(arrived, "tensor", axis=0, tiled=True),
        columns,
        (((0,), (1,)), ((), ())),
        preferred_element_type=jnp.float32,
    )
    hidden_grad = grad_sum.astype(jnp.bfloat16)[None]
    return (layer_out, gate_grad, hidden_grad)


def fused_kernel(
    routes_ref, gates_ref, out_grad_ref, hidden_hbm, weight_hbm,
    layer_ref, gate_grad_ref, hidden_grad_ref,
    hidden, weight, partial, core_out, core_in, y_out, y_in,
    slots_out, returned, tokens_out, gathered, total, terms,
    load_sem, core_send, core_recv, y_send, y_recv, out_send, out_recv,
    tok_send, tok_recv, gc_send, gc_recv, gy_send, gy_recv, gf_send, gf_recv,
    term_send, term_recv,
):
    experts, rows2, half = returned.shape
    cap = rows2 // 2
    slots = experts * cap
    own = lax.axis_index("expert")
    rank = lax.axis_index("tensor")
    chip, core = rank // 2, rank % 2
    sibling = chip * 2 + (1 - core)
    across = (1 - chip) * 2 + core
    diagonal = (1 - chip) * 2 + (1 - core)
    width = 2 * half

    def partner(i):
        index = own
        for bit in (1, 2, 4):
            if i & bit:
                index = index + bit * (1 - 2 * ((own // bit) % 2))
        return index

    def send(source, target, send_sem, recv_sem, expert, tensor):
        return pltpu.make_async_remote_copy(
            src_ref=source, dst_ref=target, send_sem=send_sem, recv_sem=recv_sem,
            device_id=(expert, tensor), device_id_type=pl.DeviceIdType.MESH,
        )

    loads = [pltpu.make_async_copy(hidden_hbm.at[0], hidden, load_sem.at[4])]
    for j, group in enumerate((diagonal, across, sibling, rank)):
        columns = pl.ds(pl.multiple_of(group * width, width), width)
        loads.append(pltpu.make_async_copy(
            weight_hbm.at[0, :, columns], weight.at[j], load_sem.at[j]))
    for load in loads[:2]:
        load.start()

    barrier = pltpu.get_barrier_semaphore()
    for i in range(1, experts):
        pl.semaphore_signal(barrier, inc=1, device_id=(partner(i), rank),
                            device_id_type=pl.DeviceIdType.MESH)
    for peer in (sibling, across, diagonal):
        pl.semaphore_signal(barrier, inc=1, device_id=(own, peer),
                            device_id_type=pl.DeviceIdType.MESH)

    def pack(values):
        left = values[:, :half].reshape(experts, cap, half)
        right = values[:, half:].reshape(experts, cap, half)
        return jnp.concatenate([left, right], axis=1)

    def unpack(values):
        values = values.astype(F32)
        both = jnp.concatenate([values[:, :cap], values[:, cap:]], axis=2)
        return both.reshape(slots, width).astype(BF16)

    routes = routes_ref[...]
    gates = gates_ref[...]
    tokens = routes.shape[1]
    expert_id = lax.broadcasted_iota(jnp.int32, (experts, tokens), 0)
    named = [(expert_id == routes[k:k + 1]).astype(F32) for k in range(2)]
    earlier = (lax.broadcasted_iota(jnp.int32, (tokens, tokens), 0)
               < lax.broadcasted_iota(jnp.int32, (tokens, tokens), 1))
    before = jnp.dot((named[0] + named[1]).astype(BF16), earlier.astype(F32).astype(BF16),
                     preferred_element_type=F32)
    slot_id = lax.broadcasted_iota(jnp.int32, (slots, tokens), 0)
    marks = []
    for k in range(2):
        position = jnp.sum(before * named[k], axis=0, keepdims=True).astype(jnp.int32)
        marks.append((slot_id == routes[k:k + 1] * cap + position).astype(F32))
    slot_gate = jnp.sum(marks[0] * gates[0:1] + marks[1] * gates[1:2], axis=1, keepdims=True)
    picked = jnp.dot((marks[0] + marks[1]).astype(BF16), out_grad_ref[...],
                     preferred_element_type=F32)
    tokens_out[...] = pack(picked * slot_gate).astype(BF16)

    for load in loads[2:]:
        load.start()

    pl.semaphore_wait(barrier, experts - 1 + 3)

    sends = []
    token_copies = {}
    for i in FAR_FIRST[:-1]:
        expert = partner(i)
        token_copies[i] = send(tokens_out.at[expert], gathered.at[0, own],
                               tok_send.at[i], tok_recv.at[i], expert, rank)
        token_copies[i].start()
    gathered[0, own] = tokens_out[own]

    to_slots, to_sibling, to_across, onward = {}, {}, {}, {}

    def share(near):
        source = partner(near)
        if near:
            token_copies[near].wait_recv()
        to_across[near] = send(gathered.at[0, source], gathered.at[2, source],
                               gy_send.at[near], gy_recv.at[near], own, across)
        to_across[near].start()
        to_sibling[near] = send(gathered.at[0, source], gathered.at[1, source],
                                gc_send.at[near], gc_recv.at[near], own, sibling)
        to_sibling[near].start()

    share(0)

    def product(j):
        return pack(jnp.dot(hidden[...], weight[j], preferred_element_type=F32))

    loads[0].wait()
    loads[1].wait()
    core_out[0] = product(0).astype(BF16)
    to_core = [send(core_out.at[n], core_in.at[n], core_send.at[n], core_recv.at[n], own, sibling)
               for n in range(2)]
    to_core[0].start()
    share(1)
    loads[2].wait()
    partial[...] = product(1)
    share(2)
    to_core[0].wait_recv()
    to_y = {}
    for i in FAR_FIRST:
        expert = partner(i)
        y_out[expert] = (partial[expert] + core_in[0, expert].astype(F32)).astype(BF16)
        to_y[i] = send(y_out.at[expert], y_in.at[expert], y_send.at[i], y_recv.at[i], own, across)
        to_y[i].start()
    loads[3].wait()
    core_out[1] = product(2).astype(BF16)
    to_core[1].start()
    share(3)
    loads[4].wait()
    partial[...] = product(3)
    to_core[1].wait_recv()
    partial[...] = partial[...] + core_in[1].astype(F32)

    for step, far in enumerate(FAR_FIRST):
        expert = partner(far)
        to_y[far].wait_recv()
        block = (partial[expert] + y_in[expert].astype(F32)).astype(BF16)
        if far:
            slots_out[expert] = block
            to_slots[far] = send(slots_out.at[expert], returned.at[own],
                                 out_send.at[far], out_recv.at[far], expert, rank)
            to_slots[far].start()
        else:
            returned[own] = block
        if step % 2:
            share(NEAR_FIRST[4 + step // 2])

    def back(part, j):
        return lax.dot_general(unpack(gathered[part]), weight[j], (((1,), (1,)), ((), ())),
                               preferred_element_type=F32)

    total[...] = back(0, 3)
    for near in NEAR_FIRST:
        to_sibling[near].wait_recv()
    total[...] = total[...] + back(1, 2)

    def pass_on(near):
        source = partner(near)
        to_across[near].wait_recv()
        onward[near] = send(gathered.at[2, source], gathered.at[3, source],
                            gf_send.at[near], gf_recv.at[near], own, sibling)
        onward[near].start()

    for near in NEAR_FIRST[:6]:
        pass_on(near)

    for far in FAR_FIRST[:-1]:
        to_slots[far].wait_recv()
    outputs = unpack(returned[...])
    cotangent = out_grad_ref[...].astype(F32)
    layer = jnp.zeros((tokens, width), F32)
    lane = lax.broadcasted_iota(jnp.int32, (tokens, tokens), 1)
    spread = jnp.zeros((tokens, tokens), F32)
    for k in range(2):
        chosen = jnp.dot(marks[k].T.astype(BF16), outputs, preferred_element_type=F32)
        gate = jnp.broadcast_to(gates[k:k + 1], (tokens, tokens)).T[:, :1]
        layer = layer + gate * chosen
        term = jnp.sum(cotangent * chosen, axis=1, keepdims=True)
        spread = spread + jnp.where(lane == k, term, 0.0)
    layer_ref[...] = layer.astype(BF16)
    terms[rank] = spread.T[:8]
    to_terms = []
    for n, peer in enumerate((sibling, across, diagonal)):
        to_terms.append(send(terms.at[rank], terms.at[rank], term_send.at[n], term_recv.at[n],
                             own, peer))
        to_terms[n].start()

    for near in NEAR_FIRST[6:]:
        pass_on(near)
    total[...] = total[...] + back(2, 1)
    for near in NEAR_FIRST:
        onward[near].wait_recv()
    hidden_grad_ref[0] = (total[...] + back(3, 0)).astype(BF16)

    for copy in to_terms:
        copy.wait_recv()
    gate_grad_ref[...] = (terms[0] + terms[1] + terms[2] + terms[3])[:2]

    for group in (token_copies, to_y, to_slots, to_sibling, to_across, onward):
        for copy in group.values():
            copy.wait_send()
    for copy in to_core + to_terms:
        copy.wait_send()


def hand_over_kernel(layer_in, gate_in, grad_in, layer_ref, gate_ref, grad_ref):
    layer_ref[...] = layer_in[...]
    gate_ref[...] = gate_in[...]
    grad_ref[...] = grad_in[...]


def hand_over(*arrays):
    vmem = pl.BlockSpec(memory_space=pltpu.VMEM)
    return pl.pallas_call(
        hand_over_kernel,
        out_shape=tuple(jax.ShapeDtypeStruct(a.shape, a.dtype) for a in arrays),
        in_specs=[vmem] * 3,
        out_specs=(vmem,) * 3,
        compiler_params=pltpu.CompilerParams(vmem_limit_bytes=16 * 1024 * 1024),
    )(*arrays)


def fused(routes, gate_weights, out_grad, hidden, down_weight):
    experts = lax.axis_size("expert")
    _, slots, depth = hidden.shape
    tokens, width = out_grad.shape
    blocks = (experts, 2 * slots // experts, width // 2)
    vmem = pl.BlockSpec(memory_space=pltpu.VMEM)
    hbm = pl.BlockSpec(memory_space=pl.ANY)
    sems = lambda n: pltpu.SemaphoreType.DMA((n,))
    layer_out, gate_grad, hidden_grad = pl.pallas_call(
        fused_kernel,
        out_shape=(
            jax.ShapeDtypeStruct((tokens, width), BF16),
            jax.ShapeDtypeStruct((2, tokens), F32),
            jax.ShapeDtypeStruct((1, slots, depth), BF16),
        ),
        in_specs=[vmem, vmem, vmem, hbm, hbm],
        out_specs=(vmem, vmem, vmem),
        scratch_shapes=[
            pltpu.VMEM((slots, depth), BF16),
            pltpu.VMEM((4, depth, width), BF16),
            pltpu.VMEM(blocks, F32),
            pltpu.VMEM((2,) + blocks, BF16),
            pltpu.VMEM((2,) + blocks, BF16),
            pltpu.VMEM(blocks, BF16),
            pltpu.VMEM(blocks, BF16),
            pltpu.VMEM(blocks, BF16),
            pltpu.VMEM(blocks, BF16),
            pltpu.VMEM(blocks, BF16),
            pltpu.VMEM((4,) + blocks, BF16),
            pltpu.VMEM((slots, depth), F32),
            pltpu.VMEM((4, 8, tokens), F32),
            sems(5), sems(2), sems(2),
        ] + [sems(8)] * 12 + [sems(3), sems(3)],
        compiler_params=pltpu.CompilerParams(
            collective_id=0, has_side_effects=True, vmem_limit_bytes=52 * 1024 * 1024
        ),
        cost_estimate=pl.CostEstimate(
            flops=16 * slots * depth * width, bytes_accessed=8 * depth * width, transcendentals=0
        ),
    )(routes.T, gate_weights.T, out_grad, hidden, down_weight)
    layer_out, gate_grad, hidden_grad = hand_over(layer_out, gate_grad, hidden_grad)
    return layer_out, gate_grad.T, hidden_grad


def per_device(routes, gate_weights, out_grad, hidden, down_weight):
    experts, ranks = lax.axis_size("expert"), lax.axis_size("tensor")
    cap = hidden.shape[1] // experts
    fits = (experts == 8 and ranks == 4 and cap % 8 == 0 and routes.shape == (128, 2)
            and out_grad.shape[1] % 256 == 0 and hidden.shape[2] % 128 == 0)
    chosen = fused if fits else plain
    return chosen(routes, gate_weights, out_grad, hidden, down_weight)


def solution(mesh):
    return jax.shard_map(
        per_device,
        mesh=mesh,
        in_specs=(
            P("expert", None),
            P("expert", None),
            P("expert", "tensor"),
            P("expert", None, "tensor"),
            P("expert", "tensor", None),
        ),
        out_specs=(P("expert", "tensor"), P("expert", None), P("expert", None, "tensor")),
        check_vma=False,
    )
```

```python
import jax
import jax.numpy as jnp
from jax import lax
from jax.experimental import pallas as pl
from jax.experimental.pallas import tpu as pltpu
from jax.sharding import PartitionSpec as P

BF16, F32 = jnp.bfloat16, jnp.float32
FAR_FIRST = (4, 5, 6, 7, 2, 3, 1, 0)
NEAR_FIRST = (0, 1, 2, 3, 6, 7, 4, 5)


def plain(routes, gate_weights, out_grad, hidden, down_weight):
    sources = lax.axis_size("expert")
    slots = hidden.shape[1]
    capacity = slots // sources
    weight = down_weight[0]
    flat = routes.reshape(-1)
    onehot = (flat[:, None] == jnp.arange(sources, dtype=jnp.int32)[None, :]).astype(jnp.int32)
    position = jnp.sum((jnp.cumsum(onehot, axis=0) - onehot) * onehot, axis=1)
    column = (flat * capacity + position).reshape(routes.shape)
    marks = column[:, :, None] == jnp.arange(slots, dtype=jnp.int32)[None, None, :]
    marks_half = marks.astype(jnp.bfloat16)
    picker = jnp.sum(marks.astype(jnp.float32), axis=1).astype(jnp.bfloat16)
    slot_gate = jnp.sum(gate_weights[:, :, None] * marks.astype(jnp.float32), axis=(0, 1))
    columns = weight
    summed = lax.psum_scatter(
        lax.dot_general(
            columns, hidden[0], (((0,), (1,)), ((), ())), preferred_element_type=jnp.float32
        ),
        "tensor",
        scatter_dimension=0,
        tiled=True,
    )
    outgoing = summed.astype(jnp.bfloat16)
    picked = lax.dot_general(
        out_grad, picker, (((0,), (0,)), ((), ())), preferred_element_type=jnp.float32
    )
    to_send = (picked * slot_gate[None, :]).astype(jnp.bfloat16)
    returned = lax.all_to_all(outgoing, "expert", split_axis=1, concat_axis=1, tiled=True)
    arrived = lax.all_to_all(to_send, "expert", split_axis=1, concat_axis=1, tiled=True)
    chosen = lax.dot_general(
        marks_half, returned, (((2,), (1,)), ((), ())), preferred_element_type=jnp.float32
    )
    layer_out = jnp.sum(gate_weights[:, :, None] * chosen, axis=1).astype(jnp.bfloat16)
    own_terms = jnp.sum(out_grad.astype(jnp.float32)[:, None, :] * chosen, axis=2)
    gate_grad = lax.psum(own_terms, "tensor")
    columns = weight
    grad_sum = lax.dot_general(
        lax.all_gather(arrived, "tensor", axis=0, tiled=True),
        columns,
        (((0,), (1,)), ((), ())),
        preferred_element_type=jnp.float32,
    )
    hidden_grad = grad_sum.astype(jnp.bfloat16)[None]
    return (layer_out, gate_grad, hidden_grad)


def fused_kernel(
    routes_ref, gates_ref, out_grad_ref, hidden_hbm, weight_hbm,
    layer_ref, gate_grad_ref, hidden_grad_ref,
    hidden, weight, partial, core_out, core_in, y_out, y_in,
    slots_out, returned, tokens_out, gathered, total, terms,
    load_sem, core_send, core_recv, y_send, y_recv, out_send, out_recv,
    tok_send, tok_recv, gc_send, gc_recv, gy_send, gy_recv, gf_send, gf_recv,
    term_send, term_recv,
):
    experts, rows2, half = returned.shape
    cap = rows2 // 2
    slots = experts * cap
    own = lax.axis_index("expert")
    rank = lax.axis_index("tensor")
    chip, core = rank // 2, rank % 2
    sibling = chip * 2 + (1 - core)
    across = (1 - chip) * 2 + core
    diagonal = (1 - chip) * 2 + (1 - core)
    width = 2 * half

    def partner(i):
        index = own
        for bit in (1, 2, 4):
            if i & bit:
                index = index + bit * (1 - 2 * ((own // bit) % 2))
        return index

    def send(source, target, send_sem, recv_sem, expert, tensor):
        return pltpu.make_async_remote_copy(
            src_ref=source, dst_ref=target, send_sem=send_sem, recv_sem=recv_sem,
            device_id=(expert, tensor), device_id_type=pl.DeviceIdType.MESH,
        )

    loads = [pltpu.make_async_copy(hidden_hbm.at[0], hidden, load_sem.at[4])]
    for j, group in enumerate((diagonal, across, sibling, rank)):
        columns = pl.ds(pl.multiple_of(group * width, width), width)
        loads.append(pltpu.make_async_copy(
            weight_hbm.at[0, :, columns], weight.at[j], load_sem.at[j]))
    for load in loads[:2]:
        load.start()

    barrier = pltpu.get_barrier_semaphore()
    for i in range(1, experts):
        pl.semaphore_signal(barrier, inc=1, device_id=(partner(i), rank),
                            device_id_type=pl.DeviceIdType.MESH)
    for peer in (sibling, across, diagonal):
        pl.semaphore_signal(barrier, inc=1, device_id=(own, peer),
                            device_id_type=pl.DeviceIdType.MESH)

    def pack(values):
        left = values[:, :half].reshape(experts, cap, half)
        right = values[:, half:].reshape(experts, cap, half)
        return jnp.concatenate([left, right], axis=1)

    def unpack(values):
        values = values.astype(F32)
        both = jnp.concatenate([values[:, :cap], values[:, cap:]], axis=2)
        return both.reshape(slots, width).astype(BF16)

    routes = routes_ref[...]
    gates = gates_ref[...]
    tokens = routes.shape[1]
    expert_id = lax.broadcasted_iota(jnp.int32, (experts, tokens), 0)
    named = [(expert_id == routes[k:k + 1]).astype(F32) for k in range(2)]
    earlier = (lax.broadcasted_iota(jnp.int32, (tokens, tokens), 0)
               < lax.broadcasted_iota(jnp.int32, (tokens, tokens), 1))
    before = jnp.dot((named[0] + named[1]).astype(BF16), earlier.astype(F32).astype(BF16),
                     preferred_element_type=F32)
    slot_id = lax.broadcasted_iota(jnp.int32, (slots, tokens), 0)
    marks = []
    for k in range(2):
        position = jnp.sum(before * named[k], axis=0, keepdims=True).astype(jnp.int32)
        marks.append((slot_id == routes[k:k + 1] * cap + position).astype(F32))
    slot_gate = jnp.sum(marks[0] * gates[0:1] + marks[1] * gates[1:2], axis=1, keepdims=True)
    picked = jnp.dot((marks[0] + marks[1]).astype(BF16), out_grad_ref[...],
                     preferred_element_type=F32)
    tokens_out[...] = pack(picked * slot_gate).astype(BF16)

    for load in loads[2:]:
        load.start()

    pl.semaphore_wait(barrier, experts - 1 + 3)

    sends = []
    token_copies = {}
    for i in FAR_FIRST[:-1]:
        expert = partner(i)
        token_copies[i] = send(tokens_out.at[expert], gathered.at[0, own],
                               tok_send.at[i], tok_recv.at[i], expert, rank)
        token_copies[i].start()
    gathered[0, own] = tokens_out[own]

    to_slots, to_sibling, to_across, onward = {}, {}, {}, {}

    def share(near):
        source = partner(near)
        if near:
            token_copies[near].wait_recv()
        to_across[near] = send(gathered.at[0, source], gathered.at[2, source],
                               gy_send.at[near], gy_recv.at[near], own, across)
        to_across[near].start()
        to_sibling[near] = send(gathered.at[0, source], gathered.at[1, source],
                                gc_send.at[near], gc_recv.at[near], own, sibling)
        to_sibling[near].start()

    share(0)

    def product(j):
        return pack(jnp.dot(hidden[...], weight[j], preferred_element_type=F32))

    loads[0].wait()
    loads[1].wait()
    core_out[0] = product(0).astype(BF16)
    to_core = [send(core_out.at[n], core_in.at[n], core_send.at[n], core_recv.at[n], own, sibling)
               for n in range(2)]
    to_core[0].start()
    share(1)
    loads[2].wait()
    partial[...] = product(1)
    to_core[0].wait_recv()
    to_y = {}
    for i in FAR_FIRST:
        expert = partner(i)
        y_out[expert] = (partial[expert] + core_in[0, expert].astype(F32)).astype(BF16)
        to_y[i] = send(y_out.at[expert], y_in.at[expert], y_send.at[i], y_recv.at[i], own, across)
        to_y[i].start()
    share(2)
    loads[3].wait()
    core_out[1] = product(2).astype(BF16)
    to_core[1].start()
    share(3)
    loads[4].wait()
    partial[...] = product(3)
    to_core[1].wait_recv()
    partial[...] = partial[...] + core_in[1].astype(F32)

    for step, far in enumerate(FAR_FIRST):
        expert = partner(far)
        to_y[far].wait_recv()
        block = (partial[expert] + y_in[expert].astype(F32)).astype(BF16)
        if far:
            slots_out[expert] = block
            to_slots[far] = send(slots_out.at[expert], returned.at[own],
                                 out_send.at[far], out_recv.at[far], expert, rank)
            to_slots[far].start()
        else:
            returned[own] = block
        if step % 2:
            share(NEAR_FIRST[4 + step // 2])

    def back(part, j):
        return lax.dot_general(unpack(gathered[part]), weight[j], (((1,), (1,)), ((), ())),
                               preferred_element_type=F32)

    total[...] = back(0, 3)
    for near in NEAR_FIRST:
        to_sibling[near].wait_recv()
    total[...] = total[...] + back(1, 2)

    def pass_on(near):
        source = partner(near)
        to_across[near].wait_recv()
        onward[near] = send(gathered.at[2, source], gathered.at[3, source],
                            gf_send.at[near], gf_recv.at[near], own, sibling)
        onward[near].start()

    for near in NEAR_FIRST[:6]:
        pass_on(near)

    for far in FAR_FIRST[:-1]:
        to_slots[far].wait_recv()
    outputs = unpack(returned[...])
    cotangent = out_grad_ref[...].astype(F32)
    layer = jnp.zeros((tokens, width), F32)
    lane = lax.broadcasted_iota(jnp.int32, (tokens, tokens), 1)
    spread = jnp.zeros((tokens, tokens), F32)
    for k in range(2):
        chosen = jnp.dot(marks[k].T.astype(BF16), outputs, preferred_element_type=F32)
        gate = jnp.broadcast_to(gates[k:k + 1], (tokens, tokens)).T[:, :1]
        layer = layer + gate * chosen
        term = jnp.sum(cotangent * chosen, axis=1, keepdims=True)
        spread = spread + jnp.where(lane == k, term, 0.0)
    layer_ref[...] = layer.astype(BF16)
    terms[rank] = spread.T[:8]
    to_terms = []
    for n, peer in enumerate((sibling, across, diagonal)):
        to_terms.append(send(terms.at[rank], terms.at[rank], term_send.at[n], term_recv.at[n],
                             own, peer))
        to_terms[n].start()

    for near in NEAR_FIRST[6:]:
        pass_on(near)
    total[...] = total[...] + back(2, 1)
    for near in NEAR_FIRST:
        onward[near].wait_recv()
    hidden_grad_ref[0] = (total[...] + back(3, 0)).astype(BF16)

    for copy in to_terms:
        copy.wait_recv()
    gate_grad_ref[...] = (terms[0] + terms[1] + terms[2] + terms[3])[:2]

    for group in (token_copies, to_y, to_slots, to_sibling, to_across, onward):
        for copy in group.values():
            copy.wait_send()
    for copy in to_core + to_terms:
        copy.wait_send()


def hand_over_kernel(layer_in, gate_in, grad_in, layer_ref, gate_ref, grad_ref):
    layer_ref[...] = layer_in[...]
    gate_ref[...] = gate_in[...]
    grad_ref[...] = grad_in[...]


def hand_over(*arrays):
    vmem = pl.BlockSpec(memory_space=pltpu.VMEM)
    return pl.pallas_call(
        hand_over_kernel,
        out_shape=tuple(jax.ShapeDtypeStruct(a.shape, a.dtype) for a in arrays),
        in_specs=[vmem] * 3,
        out_specs=(vmem,) * 3,
        compiler_params=pltpu.CompilerParams(vmem_limit_bytes=16 * 1024 * 1024),
    )(*arrays)


def fused(routes, gate_weights, out_grad, hidden, down_weight):
    experts = lax.axis_size("expert")
    _, slots, depth = hidden.shape
    tokens, width = out_grad.shape
    blocks = (experts, 2 * slots // experts, width // 2)
    vmem = pl.BlockSpec(memory_space=pltpu.VMEM)
    hbm = pl.BlockSpec(memory_space=pl.ANY)
    sems = lambda n: pltpu.SemaphoreType.DMA((n,))
    layer_out, gate_grad, hidden_grad = pl.pallas_call(
        fused_kernel,
        out_shape=(
            jax.ShapeDtypeStruct((tokens, width), BF16),
            jax.ShapeDtypeStruct((2, tokens), F32),
            jax.ShapeDtypeStruct((1, slots, depth), BF16),
        ),
        in_specs=[vmem, vmem, vmem, hbm, hbm],
        out_specs=(vmem, vmem, vmem),
        scratch_shapes=[
            pltpu.VMEM((slots, depth), BF16),
            pltpu.VMEM((4, depth, width), BF16),
            pltpu.VMEM(blocks, F32),
            pltpu.VMEM((2,) + blocks, BF16),
            pltpu.VMEM((2,) + blocks, BF16),
            pltpu.VMEM(blocks, BF16),
            pltpu.VMEM(blocks, BF16),
            pltpu.VMEM(blocks, BF16),
            pltpu.VMEM(blocks, BF16),
            pltpu.VMEM(blocks, BF16),
            pltpu.VMEM((4,) + blocks, BF16),
            pltpu.VMEM((slots, depth), F32),
            pltpu.VMEM((4, 8, tokens), F32),
            sems(5), sems(2), sems(2),
        ] + [sems(8)] * 12 + [sems(3), sems(3)],
        compiler_params=pltpu.CompilerParams(
            collective_id=0, has_side_effects=True, vmem_limit_bytes=52 * 1024 * 1024
        ),
        cost_estimate=pl.CostEstimate(
            flops=16 * slots * depth * width, bytes_accessed=8 * depth * width, transcendentals=0
        ),
    )(routes.T, gate_weights.T, out_grad, hidden, down_weight)
    layer_out, gate_grad, hidden_grad = hand_over(layer_out, gate_grad, hidden_grad)
    return layer_out, gate_grad.T, hidden_grad


def per_device(routes, gate_weights, out_grad, hidden, down_weight):
    experts, ranks = lax.axis_size("expert"), lax.axis_size("tensor")
    cap = hidden.shape[1] // experts
    fits = (experts == 8 and ranks == 4 and cap % 8 == 0 and routes.shape == (128, 2)
            and out_grad.shape[1] % 256 == 0 and hidden.shape[2] % 128 == 0)
    chosen = fused if fits else plain
    return chosen(routes, gate_weights, out_grad, hidden, down_weight)


def solution(mesh):
    return jax.shard_map(
        per_device,
        mesh=mesh,
        in_specs=(
            P("expert", None),
            P("expert", None),
            P("expert", "tensor"),
            P("expert", None, "tensor"),
            P("expert", "tensor", None),
        ),
        out_specs=(P("expert", "tensor"), P("expert", None), P("expert", None, "tensor")),
        check_vma=False,
    )
```
